512 devices in a mesh: ctx: 32 (over z, y_lo), ch: 16 (over x, y_hi, core).
Axes of the slice: x: 4, y: 8 (y_hi: 2, y_lo: 4; y = y_hi * 4 + y_lo), z: 8, core: 2. Of those that a mesh axis runs over, the one named last changes fastest.
Arguments:
- gate_stream: bfloat16 [8192, 4096], P('ctx', 'ch'), may hold values from -6 to 6
- key_stream: bfloat16 [8192, 4096], P('ctx', 'ch'), may hold values from -4 to 4
- value_stream: bfloat16 [8192, 4096], P('ctx', 'ch'), may hold values from -4 to 4
- filters: float32 [8192, 4096], P('ctx', 'ch'), may hold values from -4 to 4
- skip_gain: float32 [4096], P('ch'), may hold values from -3 to 3
- out_weight: bfloat16 [4096, 4096], P('ch'), may hold values from -0.125 to 0.125
Outputs:
- block_out: bfloat16 [8192, 4096], P('ctx', 'ch')
The draws below stay inside these ranges and needn't reach their ends.
All inputs are finite; a program needn't handle non-finite values.
Results may differ from the reference program's by a relative error of at most 0.024.
Values may be sent and summed in bfloat16 or wider, within the bound.
A program may use at most 64 MiB of HBM per device.

```python
import math
import jax
import jax.numpy as jnp
from jax import lax

C = 4096
TOKENS = 8192
N_CH = 16


def shared_normal(key):
    return jnp.clip(jax.random.normal(key, (TOKENS, C), jnp.float32), -4.0, 4.0)


def draw_key_stream(key, part):
    common = shared_normal(key)
    return common.astype(jnp.bfloat16)


def draw_value_stream(key, part):
    common = shared_normal(key)
    key = jax.random.fold_in(key, 5)
    fresh_noise = jnp.clip(jax.random.normal(key, (TOKENS, C), jnp.float32), -4.0, 4.0)
    portion = 0.6
    rest = math.sqrt(1.0 - portion * portion)
    return jnp.clip(portion * common + rest * fresh_noise, -4.0, 4.0).astype(jnp.bfloat16)


def draw_filters(key, part):
    key = jax.random.fold_in(key, 7)
    noise_key, rate_key, floor_key = jax.random.split(key, 3)
    length = TOKENS * 1.0
    lows = math.log(40.0)
    noise = jnp.clip(jax.random.normal(noise_key, (TOKENS, C), jnp.float32), -4.0, 4.0)
    spans = jnp.exp(jax.random.uniform(rate_key, (C,), jnp.float32, lows, math.log(16.0 * length)))
    steps = jnp.arange(TOKENS, dtype=jnp.float32)[:, None]
    envelope = jnp.exp(-steps / spans[None, :])
    energy = (1.0 - jnp.exp(-2.0 * length / spans)) / (1.0 - jnp.exp(-2.0 / spans))
    floor_level = jax.random.uniform(floor_key, (C,), jnp.float32, 0.4, 1.6) / length
    return noise * envelope / jnp.sqrt(energy)[None, :] + floor_level[None, :]


def strengthened(entries, rng, source, target, shards_of, factor):
    owner, partner = [(jnp.arange(entries.shape[axis_at]) // (entries.shape[axis_at] // shards_of)).reshape([-1 if axis == axis_at else 1 for axis in range(entries.ndim)]) for axis_at in (source, target)]
    chosen = jax.random.permutation(rng, shards_of)[partner]
    strong = (owner == chosen) | (owner == (partner + shards_of // 2) % shards_of)
    return jnp.where(strong, factor * entries, entries)


def level_of(stream_key, shape, cuts, least, high):
    level = 1.0
    for dim, shards_of in cuts:
        heights = jax.random.uniform(jax.random.fold_in(jax.random.fold_in(stream_key, 6), dim), (shards_of,), jnp.float32, least / len(cuts), high / len(cuts))
        level = level * jnp.repeat(jnp.exp(heights), shape[dim] // shards_of).reshape((-1,) + (1,) * (len(shape) - 1 - dim))
    return level


def normal_values(key, shape, scale, bound, cuts=(), kind=jnp.bfloat16):
    result = scale * jax.random.normal(key, shape, jnp.float32)
    if cuts:
        result = result * level_of(key, shape, cuts, -0.22, 0.18)
    return jnp.clip(result, -bound, bound).astype(kind)


def noise_with(stream_key, dims, spread, limit, cuts, heavy, held_as=jnp.bfloat16):
    entries = spread * jax.random.normal(stream_key, dims, jnp.float32)
    if cuts:
        entries = entries * level_of(stream_key, dims, cuts, -0.22, 0.18)
    return jnp.clip(strengthened(entries, jax.random.fold_in(stream_key, 3), *heavy), -limit, limit).astype(held_as)


def setup_inputs(seed: int = 0) -> dict:
    streams_of = jax.random.split(jax.random.key(seed), 7)
    gate_stream = normal_values(streams_of[0], (TOKENS, C), 1.0, 6.0, ((0, 32), (1, 16)))
    key_stream = draw_key_stream(jax.random.fold_in(streams_of[6], 71), 0)
    value_stream = draw_value_stream(jax.random.fold_in(streams_of[6], 71), 0)
    filters = draw_filters(jax.random.fold_in(streams_of[6], 71), 0)
    skip_gain = normal_values(streams_of[4], (C,), 1.0, 3.0, ((0, 16),), jnp.float32)
    out_weight = noise_with(streams_of[5], (C, C), C ** -0.5, 0.125, ((0, 16),), (0, 1, 16, 2.0))
    return {"gate_stream": gate_stream, "key_stream": key_stream, "value_stream": value_stream, "filters": filters, "skip_gain": skip_gain, "out_weight": out_weight}


def reference(gate_stream, key_stream, value_stream, filters, skip_gain, out_weight):
    mixed = key_stream.astype(jnp.float32) * value_stream.astype(jnp.float32)
    length = 2 * TOKENS
    signal_spec = jnp.fft.rfft(mixed, n=length, axis=0)
    filter_spec = jnp.fft.rfft(filters, n=length, axis=0)
    conv = jnp.fft.irfft(signal_spec * filter_spec, n=length, axis=0)[:TOKENS]
    summed = conv + skip_gain[None, :] * mixed
    gated = (gate_stream.astype(summed.dtype) * summed).astype(jnp.bfloat16)
    width = C // N_CH
    gated_slabs = jnp.transpose(gated.reshape(TOKENS, N_CH, width), (1, 0, 2))
    weight_slabs = out_weight.reshape(N_CH, width, C)

    def add_slab(total, pieces):
        term = jnp.dot(pieces[0], pieces[1], preferred_element_type=jnp.float32)
        rounded = lax.optimization_barrier(term.astype(jnp.bfloat16))
        return total + rounded.astype(total.dtype), None

    start = jnp.zeros((TOKENS, C), conv.dtype)
    total, _ = lax.scan(add_slab, start, (gated_slabs, weight_slabs))
    return total.astype(jnp.bfloat16)
```

```python
import functools
import math

import jax
import jax.numpy as jnp
import numpy as np
from jax import lax
from jax.experimental import pallas as pl
from jax.experimental.pallas import tpu as pltpu
from jax.sharding import PartitionSpec as P

MESH = pl.DeviceIdType.MESH
F32 = jnp.float32
BF16 = jnp.bfloat16

CTX = 32
ROWS = 256
WIDTH = 256
OWN = WIDTH // CTX
NX = 4
TILE = 4


def tables():
    freq = np.arange(ROWS) + 0.5
    pos = np.arange(2 * ROWS)
    theta = 2.0 * math.pi * pos[:, None] * freq[None, :] / (2 * ROWS)
    forward = np.concatenate([np.cos(theta[:ROWS]), -np.sin(theta[:ROWS])], axis=1)
    backward = np.concatenate([np.cos(theta.T), -np.sin(theta.T)], axis=0) / ROWS
    return forward.astype(BF16), backward.astype(BF16)


def kernel(
    gate_hbm, key_hbm, value_hbm, filters_hbm, skip_hbm, weight_hbm, fwd_hbm, bwd_hbm,
    out_ref,
    gate, key, value, filters, skip, fwd, bwd,
    mixed, send1, recv1, sig, fil, prod, send2, recv2,
    gated, weight, part, got, ypart, ygot,
    in_sem, w_sem, wsend_sem, wrecv_sem, send_sem, recv_sem, gsend_sem, grecv_sem,
    xsend_sem, xrecv_sem, ysend_sem, yrecv_sem,
):
    c = lax.axis_index("ctx")
    h = lax.axis_index("ch")
    x = h // 4
    yhi = (h // 2) % 2
    core = h % 2
    sibling = (c, h + 1 - 2 * core)
    across = (c, h + 2 - 4 * yhi)

    def along_x(d):
        return (c, ((x + d) % NX) * 4 + yhi * 2 + core)

    loads = []
    for i, (src, dst) in enumerate(
        [(key_hbm, key), (value_hbm, value), (filters_hbm, filters), (fwd_hbm, fwd),
         (bwd_hbm, bwd), (gate_hbm, gate), (skip_hbm, skip)]
    ):
        load = pltpu.make_async_copy(src, dst, in_sem.at[i])
        load.start()
        loads.append(load)

    barrier = pltpu.get_barrier_semaphore()

    def greet(k, carry):
        pl.semaphore_signal(barrier, inc=1, device_id=((c + k) % CTX, h), device_id_type=MESH)
        return carry

    lax.fori_loop(1, CTX, greet, 0)
    others = [sibling, across] + [along_x(d) for d in range(1, NX)]
    for dev in others:
        pl.semaphore_signal(barrier, inc=1, device_id=dev, device_id_type=MESH)

    own_w = []
    for i in range(2 * NX):
        copy = pltpu.make_async_copy(
            weight_hbm.at[:, pl.ds(pl.multiple_of((2 * i + core) * WIDTH, WIDTH), WIDTH)],
            weight.at[i, pl.ds(0, WIDTH)],
            w_sem,
        )
        copy.start()

    loads[0].wait()
    loads[1].wait()
    mixed[...] = key[...].astype(F32) * value[...].astype(F32)
    loads[2].wait()
    mixed_t = mixed[...].T.reshape(CTX, OWN, ROWS)
    filters_t = filters[...].T.reshape(CTX, OWN, ROWS)
    send1[...] = jnp.concatenate([mixed_t, filters_t], axis=1).astype(BF16)
    recv1[c] = send1[c]

    pl.semaphore_wait(barrier, CTX - 1 + len(others))

    def scatter1(k, carry):
        to = (c + k) % CTX
        pltpu.make_async_remote_copy(
            src_ref=send1.at[to], dst_ref=recv1.at[c], send_sem=send_sem.at[0],
            recv_sem=recv_sem.at[0], device_id=(to, h), device_id_type=MESH,
        ).start()
        return carry

    lax.fori_loop(1, CTX, scatter1, 0)

    for i in range(2 * NX):
        pltpu.make_async_remote_copy(
            src_ref=weight_hbm.at[:, pl.ds(pl.multiple_of((2 * i + 1 - core) * WIDTH, WIDTH), WIDTH)],
            dst_ref=weight.at[i, pl.ds(WIDTH, WIDTH)],
            send_sem=wsend_sem, recv_sem=wrecv_sem, device_id=sibling, device_id_type=MESH,
        ).start()

    loads[3].wait()
    fil[:, 0:TILE] = jnp.zeros((3, TILE, OWN, ROWS), F32)
    wait1 = pltpu.make_async_remote_copy(
        src_ref=send1.at[pl.ds(0, CTX - 1)], dst_ref=recv1.at[pl.ds(0, CTX - 1)],
        send_sem=send_sem.at[0], recv_sem=recv_sem.at[0], device_id=sibling, device_id_type=MESH,
    )
    wait1.wait_recv()

    def transform(g, carry):
        block = recv1[pl.ds(8 * g, 8)].reshape(8 * 2 * OWN, ROWS)
        spec = jnp.dot(block, fwd[...], preferred_element_type=F32).reshape(8, 2 * OWN, 2 * ROWS)
        for ref, start, first in ((sig, 0, 0), (fil, TILE, OWN)):
            real = spec[:, first : first + OWN, :ROWS]
            imag = spec[:, first : first + OWN, ROWS:]
            ref[0, pl.ds(start + 8 * g, 8)] = real
            ref[1, pl.ds(start + 8 * g, 8)] = imag
            ref[2, pl.ds(start + 8 * g, 8)] = real + imag
        return carry

    lax.fori_loop(0, CTX // 8, transform, 0)

    for n in range(CTX // TILE):
        def step(t, sums):
            sums = list(sums)
            for p in range(3):
                for q in range(2):
                    lanes = slice(128 * q, 128 * q + 128)
                    left = [sig[p, TILE * t + j, :, lanes] for j in range(TILE)]
                    right = [
                        fil[p, TILE + TILE * (n - t) + d, :, lanes] for d in range(1 - TILE, TILE)
                    ]
                    for i in range(TILE):
                        at = (p * 2 + q) * TILE + i
                        for j in range(TILE):
                            sums[at] = sums[at] + left[j] * right[i - j + TILE - 1]
            return tuple(sums)

        zero = jnp.zeros((OWN, 128), F32)
        sums = lax.fori_loop(0, n + 1, step, (zero,) * (6 * TILE))
        for q in range(2):
            one, two, three = (
                jnp.concatenate(sums[(p * 2 + q) * TILE : (p * 2 + q + 1) * TILE], axis=0)
                for p in range(3)
            )
            rows = slice(TILE * OWN * n, TILE * OWN * (n + 1))
            prod[rows, 128 * q : 128 * q + 128] = (one - two).astype(BF16)
            prod[rows, ROWS + 128 * q : ROWS + 128 * q + 128] = (three - one - two).astype(BF16)

    loads[4].wait()
    back = jnp.dot(prod[...], bwd[...], preferred_element_type=F32).reshape(CTX, OWN, 2 * ROWS)
    tail = jnp.concatenate([jnp.zeros((1, OWN, ROWS), F32), back[:-1, :, ROWS:]], axis=0)
    conv = back[:, :, :ROWS] + tail
    send2[...] = jnp.concatenate([conv[:, :, :128], conv[:, :, 128:]], axis=1).astype(BF16)
    recv2[c] = send2[c]

    def scatter2(k, carry):
        to = (c + k) % CTX
        pltpu.make_async_remote_copy(
            src_ref=send2.at[to], dst_ref=recv2.at[c], send_sem=send_sem.at[1],
            recv_sem=recv_sem.at[1], device_id=(to, h), device_id_type=MESH,
        ).start()
        return carry

    lax.fori_loop(1, CTX, scatter2, 0)
    loads[5].wait()
    loads[6].wait()
    wait2 = pltpu.make_async_remote_copy(
        src_ref=send2.at[pl.ds(0, CTX - 1)], dst_ref=recv2.at[pl.ds(0, CTX - 1)],
        send_sem=send_sem.at[1], recv_sem=recv_sem.at[1], device_id=sibling, device_id_type=MESH,
    )
    wait2.wait_recv()

    back2 = recv2[...].astype(F32)
    for half in range(2):
        conv_t = back2[:, OWN * half : OWN * (half + 1), :].reshape(WIDTH, 128).T
        rows = slice(128 * half, 128 * half + 128)
        summed = conv_t + skip[...] * mixed[rows, :]
        gated[rows, 0:WIDTH] = (gate[rows, :].astype(F32) * summed).astype(BF16)

    share = pltpu.make_async_remote_copy(
        src_ref=gated.at[:, pl.ds(0, WIDTH)], dst_ref=gated.at[:, pl.ds(WIDTH, WIDTH)],
        send_sem=gsend_sem, recv_sem=grecv_sem, device_id=sibling, device_id_type=MESH,
    )
    share.start()
    pltpu.make_async_copy(weight.at[:, pl.ds(0, WIDTH)], weight.at[:, pl.ds(0, WIDTH)], w_sem).wait()
    waitw = pltpu.make_async_remote_copy(
        src_ref=weight.at[:, pl.ds(0, WIDTH)], dst_ref=weight.at[:, pl.ds(WIDTH, WIDTH)],
        send_sem=wsend_sem, recv_sem=wrecv_sem, device_id=sibling, device_id_type=MESH,
    )
    waitw.wait_recv()
    share.wait_recv()

    def block(d, y):
        return jnp.dot(
            gated[...], weight[((x + d) % NX) * 2 + y], preferred_element_type=F32
        )

    order = (2, 1, 3)
    xcopies = {}
    for s, y in enumerate((1 - yhi, yhi)):
        for k, d in enumerate(order):
            part[s, k] = block(d, y).astype(BF16)
            copy = pltpu.make_async_remote_copy(
                src_ref=part.at[s, k], dst_ref=got.at[s, k], send_sem=xsend_sem.at[s, k],
                recv_sem=xrecv_sem.at[s, k], device_id=along_x(d), device_id_type=MESH,
            )
            copy.start()
            xcopies[s, k] = copy

    total = block(0, 1 - yhi)
    for k in range(NX - 1):
        xcopies[0, k].wait_recv()
        total = total + got[0, k].astype(F32)
    ypart[...] = total.astype(BF16)
    ycopy = pltpu.make_async_remote_copy(
        src_ref=ypart, dst_ref=ygot, send_sem=ysend_sem, recv_sem=yrecv_sem,
        device_id=across, device_id_type=MESH,
    )
    ycopy.start()
    total = block(0, yhi)
    for k in range(NX - 1):
        xcopies[1, k].wait_recv()
        total = total + got[1, k].astype(F32)
    ycopy.wait_recv()
    out_ref[...] = (total + ygot[...].astype(F32)).astype(BF16)

    wait1.wait_send()
    wait2.wait_send()
    waitw.wait_send()
    share.wait_send()
    for copy in xcopies.values():
        copy.wait_send()
    ycopy.wait_send()


def per_device(gate_stream, key_stream, value_stream, filters, skip_gain, out_weight):
    fwd, bwd = tables()
    any_spec = pl.BlockSpec(memory_space=pl.ANY)
    dma = pltpu.SemaphoreType.DMA
    return pl.pallas_call(
        kernel,
        name="hyena",
        out_shape=jax.ShapeDtypeStruct((ROWS, WIDTH), BF16),
        in_specs=[any_spec] * 8,
        out_specs=pl.BlockSpec(memory_space=pltpu.VMEM),
        scratch_shapes=[
            pltpu.VMEM((ROWS, WIDTH), BF16),
            pltpu.VMEM((ROWS, WIDTH), BF16),
            pltpu.VMEM((ROWS, WIDTH), BF16),
            pltpu.VMEM((ROWS, WIDTH), F32),
            pltpu.VMEM((1, WIDTH), F32),
            pltpu.VMEM((ROWS, 2 * ROWS), BF16),
            pltpu.VMEM((2 * ROWS, 2 * ROWS), BF16),
            pltpu.VMEM((ROWS, WIDTH), F32),
            pltpu.VMEM((CTX, 2 * OWN, ROWS), BF16),
            pltpu.VMEM((CTX, 2 * OWN, ROWS), BF16),
            pltpu.VMEM((3, CTX, OWN, ROWS), F32),
            pltpu.VMEM((3, TILE + CTX, OWN, ROWS), F32),
            pltpu.VMEM((CTX * OWN, 2 * ROWS), BF16),
            pltpu.VMEM((CTX, 2 * OWN, 128), BF16),
            pltpu.VMEM((CTX, 2 * OWN, 128), BF16),
            pltpu.VMEM((ROWS, 2 * WIDTH), BF16),
            pltpu.VMEM((2 * NX, 2 * WIDTH, WIDTH), BF16),
            pltpu.VMEM((2, NX - 1, ROWS, WIDTH), BF16),
            pltpu.VMEM((2, NX - 1, ROWS, WIDTH), BF16),
            pltpu.VMEM((ROWS, WIDTH), BF16),
            pltpu.VMEM((ROWS, WIDTH), BF16),
            dma((7,)), dma, dma, dma, dma((2,)), dma((2,)), dma, dma,
            dma((2, NX - 1)), dma((2, NX - 1)), dma, dma,
        ],
        compiler_params=pltpu.CompilerParams(
            collective_id=0, has_side_effects=True, vmem_limit_bytes=48 << 20
        ),
    )(
        gate_stream, key_stream, value_stream, filters, skip_gain[None, :], out_weight,
        jnp.asarray(fwd), jnp.asarray(bwd),
    )


def solution(mesh):
    return jax.shard_map(
        per_device,
        mesh=mesh,
        in_specs=(
            P("ctx", "ch"),
            P("ctx", "ch"),
            P("ctx", "ch"),
            P("ctx", "ch"),
            P("ch"),
            P("ch", None),
        ),
        out_specs=P("ctx", "ch"),
        check_vma=False,
    )
```

```python
import functools
import math

import jax
import jax.numpy as jnp
import numpy as np
from jax import lax
from jax.experimental import pallas as pl
from jax.experimental.pallas import tpu as pltpu
from jax.sharding import PartitionSpec as P

MESH = pl.DeviceIdType.MESH
F32 = jnp.float32
BF16 = jnp.bfloat16

CTX = 32
ROWS = 256
WIDTH = 256
OWN = WIDTH // CTX
NX = 4
CHUNKS = 4
TILE = 4


def tables():
    freq = np.arange(ROWS) + 0.5
    pos = np.arange(2 * ROWS)
    theta = 2.0 * math.pi * pos[:, None] * freq[None, :] / (2 * ROWS)
    forward = np.concatenate([np.cos(theta[:ROWS]), -np.sin(theta[:ROWS])], axis=1)
    backward = np.concatenate([np.cos(theta.T), -np.sin(theta.T)], axis=0) / ROWS
    return forward.astype(BF16), backward.astype(BF16)


def kernel(
    gate_hbm, key_hbm, value_hbm, filters_hbm, skip_hbm, weight_hbm, fwd_hbm, bwd_hbm,
    out_ref,
    gate, key, value, filters, skip, fwd, bwd,
    mixed, send1, recv1, sig, fil, send2, recv2,
    gated, weight, part, got, own, ypart, ygot,
    in_sem, w_sem, wsend_sem, wrecv_sem, send_sem, recv_sem, recv2_sem, gsend_sem, grecv_sem,
    xsend_sem, xrecv_sem, ysend_sem, yrecv_sem,
):
    c = lax.axis_index("ctx")
    h = lax.axis_index("ch")
    x = h // 4
    yhi = (h // 2) % 2
    core = h % 2
    sibling = (c, h + 1 - 2 * core)
    across = (c, h + 2 - 4 * yhi)

    def along_x(d):
        return (c, ((x + d) % NX) * 4 + yhi * 2 + core)

    loads = []
    for i, (src, dst) in enumerate(
        [(key_hbm, key), (value_hbm, value), (filters_hbm, filters), (fwd_hbm, fwd),
         (bwd_hbm, bwd), (gate_hbm, gate), (skip_hbm, skip)]
    ):
        load = pltpu.make_async_copy(src, dst, in_sem.at[i])
        load.start()
        loads.append(load)

    barrier = pltpu.get_barrier_semaphore()

    def greet(k, carry):
        pl.semaphore_signal(barrier, inc=1, device_id=((c + k) % CTX, h), device_id_type=MESH)
        return carry

    lax.fori_loop(1, CTX, greet, 0, unroll=True)
    others = [sibling, across] + [along_x(d) for d in range(1, NX)]
    for dev in others:
        pl.semaphore_signal(barrier, inc=1, device_id=dev, device_id_type=MESH)

    for i in range(2 * NX):
        copy = pltpu.make_async_copy(
            weight_hbm.at[:, pl.ds(pl.multiple_of((2 * i + core) * WIDTH, WIDTH), WIDTH)],
            weight.at[i, pl.ds(0, WIDTH)],
            w_sem,
        )
        copy.start()

    loads[0].wait()
    loads[1].wait()
    mixed[...] = key[...].astype(F32) * value[...].astype(F32)
    loads[2].wait()
    mixed_t = mixed[...].T.reshape(CTX, OWN, ROWS)
    filters_t = filters[...].T.reshape(CTX, OWN, ROWS)
    send1[...] = jnp.concatenate([mixed_t, filters_t], axis=1).astype(BF16)
    pltpu.make_async_copy(send1.at[c], recv1.at[c], recv_sem.at[c // TILE]).start()

    pl.semaphore_wait(barrier, CTX - 1 + len(others))

    def scatter1(k, carry):
        to = (c + k) % CTX
        pltpu.make_async_remote_copy(
            src_ref=send1.at[to], dst_ref=recv1.at[c], send_sem=send_sem.at[0],
            recv_sem=recv_sem.at[c // TILE], device_id=(to, h), device_id_type=MESH,
        ).start()
        return carry

    lax.fori_loop(1, CTX, scatter1, 0, unroll=True)

    for i in range(2 * NX):
        pltpu.make_async_remote_copy(
            src_ref=weight_hbm.at[:, pl.ds(pl.multiple_of((2 * i + 1 - core) * WIDTH, WIDTH), WIDTH)],
            dst_ref=weight.at[i, pl.ds(WIDTH, WIDTH)],
            send_sem=wsend_sem, recv_sem=wrecv_sem, device_id=sibling, device_id_type=MESH,
        ).start()

    loads[3].wait()
    fil[:, 0:TILE] = jnp.zeros((3, TILE, OWN, ROWS), F32)
    last = jnp.zeros((1, OWN, ROWS), F32)
    for n in range(CTX // TILE):
        tile = pl.ds(TILE * n, TILE)
        pltpu.make_async_copy(send1.at[tile], recv1.at[tile], recv_sem.at[n]).wait()
        spec = jnp.dot(
            recv1[tile].reshape(TILE * 2 * OWN, ROWS), fwd[...], preferred_element_type=F32
        ).reshape(TILE, 2 * OWN, 2 * ROWS)
        for ref, start, low in ((sig, 0, 0), (fil, TILE, OWN)):
            real = spec[:, low : low + OWN, :ROWS]
            imag = spec[:, low : low + OWN, ROWS:]
            ref[0, pl.ds(start + TILE * n, TILE)] = real
            ref[1, pl.ds(start + TILE * n, TILE)] = imag
            ref[2, pl.ds(start + TILE * n, TILE)] = real + imag

        def step(t, sums):
            sums = list(sums)
            for p in range(3):
                for q in range(2):
                    lanes = slice(128 * q, 128 * q + 128)
                    left = [sig[p, TILE * t + j, :, lanes] for j in range(TILE)]
                    right = [
                        fil[p, TILE + TILE * (n - t) + d, :, lanes] for d in range(1 - TILE, TILE)
                    ]
                    for i in range(TILE):
                        at = (p * 2 + q) * TILE + i
                        for j in range(TILE):
                            sums[at] = sums[at] + left[j] * right[i - j + TILE - 1]
            return tuple(sums)

        zero = jnp.zeros((OWN, 128), F32)
        sums = lax.fori_loop(0, n + 1, step, (zero,) * (6 * TILE))
        one, two, three = (
            jnp.concatenate(
                [jnp.concatenate(sums[(2 * p + q) * TILE : (2 * p + q + 1) * TILE], axis=0) for q in range(2)],
                axis=1,
            )
            for p in range(3)
        )
        prod = jnp.concatenate([one - two, three - one - two], axis=1).astype(BF16)
        if n == 0:
            loads[4].wait()
        back = jnp.dot(prod, bwd[...], preferred_element_type=F32).reshape(TILE, OWN, 2 * ROWS)
        conv = back[:, :, :ROWS] + jnp.concatenate([last, back[:-1, :, ROWS:]], axis=0)
        last = back[TILE - 1 :, :, ROWS:]
        send2[tile] = jnp.concatenate([conv[:, :, :128], conv[:, :, 128:]], axis=1).astype(BF16)
        for to in range(TILE * n, TILE * (n + 1)):
            @pl.when(to != c)
            def _():
                pltpu.make_async_remote_copy(
                    src_ref=send2.at[to], dst_ref=recv2.at[c], send_sem=send_sem.at[1],
                    recv_sem=recv2_sem, device_id=(to, h), device_id_type=MESH,
                ).start()

            @pl.when(to == c)
            def _():
                pltpu.make_async_copy(send2.at[to], recv2.at[c], recv2_sem).start()

    loads[5].wait()
    loads[6].wait()
    pltpu.make_async_copy(send2, recv2, recv2_sem).wait()

    back2 = recv2[...].astype(F32)
    for half in range(2):
        conv_t = back2[:, OWN * half : OWN * (half + 1), :].reshape(WIDTH, 128).T
        rows = slice(128 * half, 128 * half + 128)
        summed = conv_t + skip[...] * mixed[rows, :]
        gated[rows, 0:WIDTH] = (gate[rows, :].astype(F32) * summed).astype(BF16)

    share = pltpu.make_async_remote_copy(
        src_ref=gated.at[:, pl.ds(0, WIDTH)], dst_ref=gated.at[:, pl.ds(WIDTH, WIDTH)],
        send_sem=gsend_sem, recv_sem=grecv_sem, device_id=sibling, device_id_type=MESH,
    )
    share.start()
    pltpu.make_async_copy(weight.at[:, pl.ds(0, WIDTH)], weight.at[:, pl.ds(0, WIDTH)], w_sem).wait()
    waitw = pltpu.make_async_remote_copy(
        src_ref=weight.at[:, pl.ds(0, WIDTH)], dst_ref=weight.at[:, pl.ds(WIDTH, WIDTH)],
        send_sem=wsend_sem, recv_sem=wrecv_sem, device_id=sibling, device_id_type=MESH,
    )
    waitw.wait_recv()
    share.wait_recv()

    def block(d, y, rows=slice(None)):
        return jnp.dot(
            gated[rows], weight[((x + d) % NX) * 2 + y], preferred_element_type=F32
        )

    order = (2, 1, 3)
    step = ROWS // CHUNKS

    def send_x(s, k, r, rows):
        copy = pltpu.make_async_remote_copy(
            src_ref=part.at[s, k, rows], dst_ref=got.at[s, k, rows], send_sem=xsend_sem.at[s, k, r],
            recv_sem=xrecv_sem.at[s, k, r], device_id=along_x(order[k]), device_id_type=MESH,
        )
        copy.start()
        return copy

    first = []
    for r in range(CHUNKS):
        rows = pl.ds(step * r, step)
        for k, d in enumerate(order):
            part[0, k, rows] = block(d, 1 - yhi, rows).astype(BF16)
        first.append([send_x(0, k, r, rows) for k in range(NX - 1)])
    second = []
    for k, d in enumerate(order):
        part[1, k] = block(d, yhi).astype(BF16)
        second.append(send_x(1, k, 0, pl.ds(0, ROWS)))
    own[0] = block(0, 1 - yhi)
    own[1] = block(0, yhi)
    ycopies = []
    for r in range(CHUNKS):
        rows = pl.ds(step * r, step)
        total = own[0, rows]
        for k in range(NX - 1):
            first[r][k].wait_recv()
            total = total + got[0, k, rows].astype(F32)
        ypart[rows] = total.astype(BF16)
        copy = pltpu.make_async_remote_copy(
            src_ref=ypart.at[rows], dst_ref=ygot.at[rows], send_sem=ysend_sem.at[r],
            recv_sem=yrecv_sem.at[r], device_id=across, device_id_type=MESH,
        )
        copy.start()
        ycopies.append(copy)
    total = own[1]
    for k in range(NX - 1):
        second[k].wait_recv()
        total = total + got[1, k].astype(F32)
    own[1] = total
    for r in range(CHUNKS):
        rows = pl.ds(step * r, step)
        ycopies[r].wait_recv()
        out_ref[rows] = (own[1, rows] + ygot[rows].astype(F32)).astype(BF16)

    for n, (sent, landed) in enumerate(((send1, recv1), (send2, recv2))):
        pltpu.make_async_remote_copy(
            src_ref=sent.at[pl.ds(0, CTX - 1)], dst_ref=landed.at[pl.ds(0, CTX - 1)],
            send_sem=send_sem.at[n], recv_sem=recv2_sem, device_id=sibling, device_id_type=MESH,
        ).wait_send()
    waitw.wait_send()
    share.wait_send()
    for copy in sum(first, []) + second + ycopies:
        copy.wait_send()


def per_device(gate_stream, key_stream, value_stream, filters, skip_gain, out_weight):
    fwd, bwd = tables()
    any_spec = pl.BlockSpec(memory_space=pl.ANY)
    dma = pltpu.SemaphoreType.DMA
    return pl.pallas_call(
        kernel,
        name="hyena",
        out_shape=pltpu.VMEM((ROWS, WIDTH), BF16),
        in_specs=[any_spec] * 8,
        out_specs=pl.BlockSpec(memory_space=pltpu.VMEM),
        scratch_shapes=[
            pltpu.VMEM((ROWS, WIDTH), BF16),
            pltpu.VMEM((ROWS, WIDTH), BF16),
            pltpu.VMEM((ROWS, WIDTH), BF16),
            pltpu.VMEM((ROWS, WIDTH), F32),
            pltpu.VMEM((1, WIDTH), F32),
            pltpu.VMEM((ROWS, 2 * ROWS), BF16),
            pltpu.VMEM((2 * ROWS, 2 * ROWS), BF16),
            pltpu.VMEM((ROWS, WIDTH), F32),
            pltpu.VMEM((CTX, 2 * OWN, ROWS), BF16),
            pltpu.VMEM((CTX, 2 * OWN, ROWS), BF16),
            pltpu.VMEM((3, CTX, OWN, ROWS), F32),
            pltpu.VMEM((3, TILE + CTX, OWN, ROWS), F32),
            pltpu.VMEM((CTX, 2 * OWN, 128), BF16),
            pltpu.VMEM((CTX, 2 * OWN, 128), BF16),
            pltpu.VMEM((ROWS, 2 * WIDTH), BF16),
            pltpu.VMEM((2 * NX, 2 * WIDTH, WIDTH), BF16),
            pltpu.VMEM((2, NX - 1, ROWS, WIDTH), BF16),
            pltpu.VMEM((2, NX - 1, ROWS, WIDTH), BF16),
            pltpu.VMEM((2, ROWS, WIDTH), F32),
            pltpu.VMEM((ROWS, WIDTH), BF16),
            pltpu.VMEM((ROWS, WIDTH), BF16),
            dma((7,)), dma, dma, dma, dma((2,)), dma((CTX // TILE,)), dma, dma, dma,
            dma((2, NX - 1, CHUNKS)), dma((2, NX - 1, CHUNKS)), dma((CHUNKS,)), dma((CHUNKS,)),
        ],
        compiler_params=pltpu.CompilerParams(
            collective_id=0, has_side_effects=True, vmem_limit_bytes=56 << 20
        ),
    )(
        gate_stream, key_stream, value_stream, filters, skip_gain[None, :], out_weight,
        jnp.asarray(fwd), jnp.asarray(bwd),
    )


def solution(mesh):
    return jax.shard_map(
        per_device,
        mesh=mesh,
        in_specs=(
            P("ctx", "ch"),
            P("ctx", "ch"),
            P("ctx", "ch"),
            P("ctx", "ch"),
            P("ch"),
            P("ch", None),
        ),
        out_specs=P("ctx", "ch"),
        check_vma=False,
    )
```

```python
import functools
import math

import jax
import jax.numpy as jnp
import numpy as np
from jax import lax
from jax.experimental import pallas as pl
from jax.experimental.pallas import tpu as pltpu
from jax.sharding import PartitionSpec as P

MESH = pl.DeviceIdType.MESH
F32 = jnp.float32
BF16 = jnp.bfloat16

CTX = 32
ROWS = 256
WIDTH = 256
OWN = WIDTH // CTX
NX = 4
CHUNKS = 4
TILE = 4


def tables():
    freq = np.arange(ROWS) + 0.5
    pos = np.arange(2 * ROWS)
    theta = 2.0 * math.pi * pos[:, None] * freq[None, :] / (2 * ROWS)
    forward = np.concatenate([np.cos(theta[:ROWS]), -np.sin(theta[:ROWS])], axis=1)
    backward = np.concatenate([np.cos(theta.T), -np.sin(theta.T)], axis=0) / ROWS
    return forward.astype(BF16), backward.astype(BF16)


def kernel(
    gate_hbm, key_hbm, value_hbm, filters_hbm, skip_hbm, weight_hbm, fwd_hbm, bwd_hbm,
    out_ref,
    gate, key, value, filters, skip, fwd, bwd,
    send1, recv1, sig, fil, send2, recv2,
    gated, weight, part, got, ring, ringgot, onward, own, ypart, ygot,
    in_sem, w_sem, wsend_sem, wrecv_sem, send_sem, recv_sem, recv2_sem, gsend_sem, grecv_sem,
    xsend_sem, xrecv_sem, rsend_sem, rrecv_sem, ysend_sem, yrecv_sem,
):
    c = lax.axis_index("ctx")
    h = lax.axis_index("ch")
    x = h // 4
    yhi = (h // 2) % 2
    core = h % 2
    sibling = (c, h + 1 - 2 * core)
    across = (c, h + 2 - 4 * yhi)

    def along_x(d):
        return (c, ((x + d) % NX) * 4 + yhi * 2 + core)

    loads = []
    for i, (src, dst) in enumerate(
        [(key_hbm, key.at[0]), (value_hbm, value.at[0]), (filters_hbm, filters), (fwd_hbm, fwd),
         (bwd_hbm, bwd), (gate_hbm, gate.at[0]), (skip_hbm, skip.at[0])]
    ):
        load = pltpu.make_async_copy(src, dst, in_sem.at[i])
        load.start()
        loads.append(load)

    barrier = pltpu.get_barrier_semaphore()

    def greet(k, carry):
        pl.semaphore_signal(barrier, inc=1, device_id=((c + k) % CTX, h), device_id_type=MESH)
        return carry

    lax.fori_loop(1, CTX, greet, 0, unroll=True)
    others = [sibling, across] + [along_x(d) for d in range(1, NX)]
    for dev in others:
        pl.semaphore_signal(barrier, inc=1, device_id=dev, device_id_type=MESH)

    for i in range(2 * NX):
        copy = pltpu.make_async_copy(
            weight_hbm.at[:, pl.ds(pl.multiple_of((2 * i + core) * WIDTH, WIDTH), WIDTH)],
            weight.at[i, pl.ds(0, WIDTH)],
            w_sem,
        )
        copy.start()

    loads[0].wait()
    loads[1].wait()
    mixed = key[0].astype(F32) * value[0].astype(F32)
    loads[2].wait()
    mixed_t = mixed.T.reshape(CTX, OWN, ROWS)
    filters_t = filters[...].T.reshape(CTX, OWN, ROWS)
    send1[...] = jnp.concatenate([mixed_t, filters_t], axis=1).astype(BF16)
    pltpu.make_async_copy(send1.at[c], recv1.at[c], recv_sem.at[c // TILE]).start()

    pl.semaphore_wait(barrier, CTX - 1 + len(others))

    def scatter1(k, carry):
        to = (c + k) % CTX
        pltpu.make_async_remote_copy(
            src_ref=send1.at[to], dst_ref=recv1.at[c], send_sem=send_sem.at[0],
            recv_sem=recv_sem.at[c // TILE], device_id=(to, h), device_id_type=MESH,
        ).start()
        return carry

    lax.fori_loop(1, CTX, scatter1, 0, unroll=True)

    for i in range(2 * NX):
        pltpu.make_async_remote_copy(
            src_ref=weight_hbm.at[:, pl.ds(pl.multiple_of((2 * i + 1 - core) * WIDTH, WIDTH), WIDTH)],
            dst_ref=weight.at[i, pl.ds(WIDTH, WIDTH)],
            send_sem=wsend_sem, recv_sem=wrecv_sem, device_id=sibling, device_id_type=MESH,
        ).start()
    streams = [
        pltpu.make_async_remote_copy(
            src_ref=src, dst_ref=dst.at[1], send_sem=gsend_sem.at[i], recv_sem=grecv_sem.at[i],
            device_id=sibling, device_id_type=MESH,
        )
        for i, (src, dst) in enumerate(
            [(key_hbm, key), (value_hbm, value), (gate_hbm, gate), (skip_hbm, skip)]
        )
    ]
    for copy in streams:
        copy.start()

    loads[3].wait()
    fil[:, 0:TILE] = jnp.zeros((3, TILE, OWN, ROWS), F32)
    last = jnp.zeros((1, OWN, ROWS), F32)
    for n in range(CTX // TILE):
        tile = pl.ds(TILE * n, TILE)
        pltpu.make_async_copy(send1.at[tile], recv1.at[tile], recv_sem.at[n]).wait()
        spec = jnp.dot(
            recv1[tile].reshape(TILE * 2 * OWN, ROWS), fwd[...], preferred_element_type=F32
        ).reshape(TILE, 2 * OWN, 2 * ROWS)
        for ref, start, low in ((sig, 0, 0), (fil, TILE, OWN)):
            real = spec[:, low : low + OWN, :ROWS]
            imag = spec[:, low : low + OWN, ROWS:]
            ref[0, pl.ds(start + TILE * n, TILE)] = real
            ref[1, pl.ds(start + TILE * n, TILE)] = imag
            ref[2, pl.ds(start + TILE * n, TILE)] = real + imag

        def step(t, sums):
            sums = list(sums)
            for p in range(3):
                for q in range(2):
                    lanes = slice(128 * q, 128 * q + 128)
                    left = [sig[p, TILE * t + j, :, lanes] for j in range(TILE)]
                    right = [
                        fil[p, TILE + TILE * (n - t) + d, :, lanes] for d in range(1 - TILE, TILE)
                    ]
                    for i in range(TILE):
                        at = (p * 2 + q) * TILE + i
                        for j in range(TILE):
                            sums[at] = sums[at] + left[j] * right[i - j + TILE - 1]
            return tuple(sums)

        zero = jnp.zeros((OWN, 128), F32)
        sums = lax.fori_loop(0, n + 1, step, (zero,) * (6 * TILE))
        one, two, three = (
            jnp.concatenate(
                [jnp.concatenate(sums[(2 * p + q) * TILE : (2 * p + q + 1) * TILE], axis=0) for q in range(2)],
                axis=1,
            )
            for p in range(3)
        )
        prod = jnp.concatenate([one - two, three - one - two], axis=1).astype(BF16)
        if n == 0:
            loads[4].wait()
        back = jnp.dot(prod, bwd[...], preferred_element_type=F32).reshape(TILE, OWN, 2 * ROWS)
        conv = back[:, :, :ROWS] + jnp.concatenate([last, back[:-1, :, ROWS:]], axis=0)
        last = back[TILE - 1 :, :, ROWS:]
        send2[tile] = jnp.concatenate([conv[:, :, :128], conv[:, :, 128:]], axis=1).astype(BF16)
        for to in range(TILE * n, TILE * (n + 1)):
            @pl.when(to != c)
            def _():
                pltpu.make_async_remote_copy(
                    src_ref=send2.at[to], dst_ref=recv2.at[0, c], send_sem=send_sem.at[1],
                    recv_sem=recv2_sem.at[0], device_id=(to, h), device_id_type=MESH,
                ).start()

            @pl.when(to == c)
            def _():
                pltpu.make_async_copy(send2.at[to], recv2.at[0, c], recv2_sem.at[0]).start()

            pltpu.make_async_remote_copy(
                src_ref=send2.at[to], dst_ref=recv2.at[1, c], send_sem=send_sem.at[2],
                recv_sem=recv2_sem.at[1], device_id=(to, sibling[1]), device_id_type=MESH,
            ).start()


    loads[5].wait()
    loads[6].wait()
    for copy in streams:
        copy.wait_recv()
    for s in range(2):
        pltpu.make_async_copy(send2, recv2.at[s], recv2_sem.at[s]).wait()
        returned = recv2[s].astype(F32)
        for i in range(2):
            rows = slice(128 * i, 128 * i + 128)
            conv_t = returned[:, OWN * i : OWN * (i + 1), :].reshape(WIDTH, 128).T
            mixed = key[s, rows].astype(F32) * value[s, rows].astype(F32)
            summed = conv_t + skip[s] * mixed
            gated[rows, WIDTH * s : WIDTH * (s + 1)] = (gate[s, rows].astype(F32) * summed).astype(BF16)

    pltpu.make_async_copy(weight.at[:, pl.ds(0, WIDTH)], weight.at[:, pl.ds(0, WIDTH)], w_sem).wait()
    waitw = pltpu.make_async_remote_copy(
        src_ref=weight.at[:, pl.ds(0, WIDTH)], dst_ref=weight.at[:, pl.ds(WIDTH, WIDTH)],
        send_sem=wsend_sem, recv_sem=wrecv_sem, device_id=sibling, device_id_type=MESH,
    )
    waitw.wait_recv()

    def block(d, y, rows=slice(None)):
        return jnp.dot(
            gated[rows], weight[((x + d) % NX) * 2 + y], preferred_element_type=F32
        )

    order = (2, 1, 3)
    step = ROWS // CHUNKS
    half = ROWS // 2
    top, bottom = slice(0, half), slice(half, ROWS)

    def send_across(r):
        rows = pl.ds(step * r, step)
        copies = []
        for k, d in enumerate(order):
            part[k, rows] = block(d, 1 - yhi, rows).astype(BF16)
            copy = pltpu.make_async_remote_copy(
                src_ref=part.at[k, rows], dst_ref=got.at[k, rows], send_sem=xsend_sem.at[k, r],
                recv_sem=xrecv_sem.at[k, r], device_id=along_x(d), device_id_type=MESH,
            )
            copy.start()
            copies.append(copy)
        return copies

    def send_ring(i, terms):
        ring[i] = terms.astype(BF16)
        copy = pltpu.make_async_remote_copy(
            src_ref=ring.at[i], dst_ref=ringgot.at[i], send_sem=rsend_sem.at[i],
            recv_sem=rrecv_sem.at[i], device_id=along_x(3 if i % 2 else 1), device_id_type=MESH,
        )
        copy.start()
        return copy

    def arrived(i):
        ringcopies[i].wait_recv()
        return ringgot[i].astype(F32)

    first = [send_across(r) for r in range(CHUNKS)]
    far = block(2, yhi)
    ringcopies = [send_ring(0, far[top]), send_ring(1, far[bottom])]
    right, left = block(1, yhi), block(3, yhi)
    ringcopies += [send_ring(2, right[bottom]), send_ring(3, left[top])]
    onward[0] = right[top]
    onward[1] = left[bottom]
    own[0] = block(0, 1 - yhi)
    own[1] = block(0, yhi)
    ycopies = []
    for r in range(CHUNKS):
        rows = pl.ds(step * r, step)
        total = own[0, rows]
        for k in range(NX - 1):
            first[r][k].wait_recv()
            total = total + got[k, rows].astype(F32)
        ypart[rows] = total.astype(BF16)
        copy = pltpu.make_async_remote_copy(
            src_ref=ypart.at[rows], dst_ref=ygot.at[rows], send_sem=ysend_sem.at[r],
            recv_sem=yrecv_sem.at[r], device_id=across, device_id_type=MESH,
        )
        copy.start()
        ycopies.append(copy)
    ringcopies += [send_ring(4 + i, onward[i] + arrived(i)) for i in range(2)]
    own[1, top] = own[1, top] + arrived(3) + arrived(4)
    own[1, bottom] = own[1, bottom] + arrived(2) + arrived(5)
    for r in range(CHUNKS):
        rows = pl.ds(step * r, step)
        ycopies[r].wait_recv()
        out_ref[rows] = (own[1, rows] + ygot[rows].astype(F32)).astype(BF16)

    for n, count in enumerate((CTX - 1, CTX - 1, CTX)):
        sent = (send1, send2, send2)[n].at[pl.ds(0, count)]
        pltpu.make_async_remote_copy(
            src_ref=sent, dst_ref=sent, send_sem=send_sem.at[n], recv_sem=recv2_sem.at[0],
            device_id=sibling, device_id_type=MESH,
        ).wait_send()
    waitw.wait_send()
    for copy in streams + sum(first, []) + ringcopies + ycopies:
        copy.wait_send()


def per_device(gate_stream, key_stream, value_stream, filters, skip_gain, out_weight):
    fwd, bwd = tables()
    any_spec = pl.BlockSpec(memory_space=pl.ANY)
    dma = pltpu.SemaphoreType.DMA
    return pl.pallas_call(
        kernel,
        name="hyena",
        out_shape=pltpu.VMEM((ROWS, WIDTH), BF16),
        in_specs=[any_spec] * 8,
        out_specs=pl.BlockSpec(memory_space=pltpu.VMEM),
        scratch_shapes=[
            pltpu.VMEM((2, ROWS, WIDTH), BF16),
            pltpu.VMEM((2, ROWS, WIDTH), BF16),
            pltpu.VMEM((2, ROWS, WIDTH), BF16),
            pltpu.VMEM((ROWS, WIDTH), F32),
            pltpu.VMEM((2, 1, WIDTH), F32),
            pltpu.VMEM((ROWS, 2 * ROWS), BF16),
            pltpu.VMEM((2 * ROWS, 2 * ROWS), BF16),
            pltpu.VMEM((CTX, 2 * OWN, ROWS), BF16),
            pltpu.VMEM((CTX, 2 * OWN, ROWS), BF16),
            pltpu.VMEM((3, CTX, OWN, ROWS), F32),
            pltpu.VMEM((3, TILE + CTX, OWN, ROWS), F32),
            pltpu.VMEM((CTX, 2 * OWN, 128), BF16),
            pltpu.VMEM((2, CTX, 2 * OWN, 128), BF16),
            pltpu.VMEM((ROWS, 2 * WIDTH), BF16),
            pltpu.VMEM((2 * NX, 2 * WIDTH, WIDTH), BF16),
            pltpu.VMEM((NX - 1, ROWS, WIDTH), BF16),
            pltpu.VMEM((NX - 1, ROWS, WIDTH), BF16),
            pltpu.VMEM((6, ROWS // 2, WIDTH), BF16),
            pltpu.VMEM((6, ROWS // 2, WIDTH), BF16),
            pltpu.VMEM((2, ROWS // 2, WIDTH), F32),
            pltpu.VMEM((2, ROWS, WIDTH), F32),
            pltpu.VMEM((ROWS, WIDTH), BF16),
            pltpu.VMEM((ROWS, WIDTH), BF16),
            dma((7,)), dma, dma, dma, dma((3,)), dma((CTX // TILE,)), dma((2,)), dma((4,)), dma((4,)),
            dma((NX - 1, CHUNKS)), dma((NX - 1, CHUNKS)), dma((6,)), dma((6,)), dma((CHUNKS,)), dma((CHUNKS,)),
        ],
        compiler_params=pltpu.CompilerParams(
            collective_id=0, has_side_effects=True, vmem_limit_bytes=56 << 20
        ),
    )(
        gate_stream, key_stream, value_stream, filters, skip_gain[None, :], out_weight,
        jnp.asarray(fwd), jnp.asarray(bwd),
    )


def solution(mesh):
    return jax.shard_map(
        per_device,
        mesh=mesh,
        in_specs=(
            P("ctx", "ch"),
            P("ctx", "ch"),
            P("ctx", "ch"),
            P("ctx", "ch"),
            P("ch"),
            P("ch", None),
        ),
        out_specs=P("ctx", "ch"),
        check_vma=False,
    )
```

```python
import functools
import math

import jax
import jax.numpy as jnp
import numpy as np
from jax import lax
from jax.experimental import pallas as pl
from jax.experimental.pallas import tpu as pltpu
from jax.sharding import PartitionSpec as P

MESH = pl.DeviceIdType.MESH
F32 = jnp.float32
BF16 = jnp.bfloat16

CTX = 32
ROWS = 256
WIDTH = 256
OWN = WIDTH // CTX
NX = 4
CHUNKS = 4
STRIDE = 5
TILE = 4


def tables():
    freq = np.arange(ROWS) + 0.5
    pos = np.arange(2 * ROWS)
    theta = 2.0 * math.pi * pos[:, None] * freq[None, :] / (2 * ROWS)
    forward = np.concatenate([np.cos(theta[:ROWS]), -np.sin(theta[:ROWS])], axis=1)
    backward = np.concatenate([np.cos(theta.T), -np.sin(theta.T)], axis=0) / ROWS
    return forward.astype(BF16), backward.astype(BF16)


def kernel(
    gate_hbm, key_hbm, value_hbm, filters_hbm, skip_hbm, weight_hbm, fwd_hbm, bwd_hbm,
    out_ref,
    gate, key, value, filters, skip, fwd, bwd,
    send1, recv1, sig, fil, send2, recv2,
    gated, weight, part, got, ring, ringgot, onward, own, ypart, ygot,
    in_sem, w_sem, wsend_sem, wrecv_sem, send_sem, recv_sem, recv2_sem, gsend_sem, grecv_sem,
    xsend_sem, xrecv_sem, rsend_sem, rrecv_sem, ysend_sem, yrecv_sem,
):
    c = lax.axis_index("ctx")
    h = lax.axis_index("ch")
    x = h // 4
    yhi = (h // 2) % 2
    core = h % 2
    sibling = (c, h + 1 - 2 * core)
    across = (c, h + 2 - 4 * yhi)

    def along_x(d):
        return (c, ((x + d) % NX) * 4 + yhi * 2 + core)

    barrier = pltpu.get_barrier_semaphore()

    def greet(k, carry):
        pl.semaphore_signal(barrier, inc=1, device_id=((c + k) % CTX, h), device_id_type=MESH)
        return carry

    lax.fori_loop(1, CTX, greet, 0, unroll=True)
    others = [sibling, across] + [along_x(d) for d in range(1, NX)]
    for dev in others:
        pl.semaphore_signal(barrier, inc=1, device_id=dev, device_id_type=MESH)

    loads = []
    for i, (src, dst) in enumerate(
        [(key_hbm, key.at[0]), (value_hbm, value.at[0]), (filters_hbm, filters), (fwd_hbm, fwd),
         (bwd_hbm, bwd), (gate_hbm, gate.at[0]), (skip_hbm, skip.at[0])]
    ):
        load = pltpu.make_async_copy(src, dst, in_sem.at[i])
        load.start()
        loads.append(load)

    for i in range(2 * NX):
        copy = pltpu.make_async_copy(
            weight_hbm.at[:, pl.ds(pl.multiple_of((2 * i + core) * WIDTH, WIDTH), WIDTH)],
            weight.at[i, pl.ds(0, WIDTH)],
            w_sem,
        )
        copy.start()

    loads[0].wait()
    loads[1].wait()
    mixed = key[0].astype(F32) * value[0].astype(F32)
    loads[2].wait()
    mixed_t = mixed.T.reshape(CTX, OWN, ROWS)
    filters_t = filters[...].T.reshape(CTX, OWN, ROWS)
    send1[...] = jnp.concatenate([mixed_t, filters_t], axis=1).astype(BF16)
    pltpu.make_async_copy(send1.at[c], recv1.at[c], recv_sem.at[c // TILE]).start()

    pl.semaphore_wait(barrier, CTX - 1 + len(others))

    for k in range(1, CTX):
        to = (c + k * STRIDE % CTX) % CTX
        pltpu.make_async_remote_copy(
            src_ref=send1.at[to], dst_ref=recv1.at[c], send_sem=send_sem.at[0],
            recv_sem=recv_sem.at[c // TILE], device_id=(to, h), device_id_type=MESH,
        ).start()

    for i in range(2 * NX):
        pltpu.make_async_remote_copy(
            src_ref=weight_hbm.at[:, pl.ds(pl.multiple_of((2 * i + 1 - core) * WIDTH, WIDTH), WIDTH)],
            dst_ref=weight.at[i, pl.ds(WIDTH, WIDTH)],
            send_sem=wsend_sem, recv_sem=wrecv_sem, device_id=sibling, device_id_type=MESH,
        ).start()
    streams = [
        pltpu.make_async_remote_copy(
            src_ref=src, dst_ref=dst.at[1], send_sem=gsend_sem.at[i], recv_sem=grecv_sem.at[i],
            device_id=sibling, device_id_type=MESH,
        )
        for i, (src, dst) in enumerate(
            [(key_hbm, key), (value_hbm, value), (gate_hbm, gate), (skip_hbm, skip)]
        )
    ]
    for copy in streams:
        copy.start()

    loads[3].wait()
    fil[:, 0:TILE] = jnp.zeros((3, TILE, OWN, ROWS), F32)
    last = jnp.zeros((1, OWN, ROWS), F32)
    for n in range(CTX // TILE):
        tile = pl.ds(TILE * n, TILE)
        pltpu.make_async_copy(send1.at[tile], recv1.at[tile], recv_sem.at[n]).wait()
        spec = jnp.dot(
            recv1[tile].reshape(TILE * 2 * OWN, ROWS), fwd[...], preferred_element_type=F32
        ).reshape(TILE, 2 * OWN, 2 * ROWS)
        for ref, start, low in ((sig, 0, 0), (fil, TILE, OWN)):
            real = spec[:, low : low + OWN, :ROWS]
            imag = spec[:, low : low + OWN, ROWS:]
            ref[0, pl.ds(start + TILE * n, TILE)] = real
            ref[1, pl.ds(start + TILE * n, TILE)] = imag
            ref[2, pl.ds(start + TILE * n, TILE)] = real + imag

        def step(t, sums):
            sums = list(sums)
            for p in range(3):
                for q in range(2):
                    lanes = slice(128 * q, 128 * q + 128)
                    left = [sig[p, TILE * t + j, :, lanes] for j in range(TILE)]
                    right = [
                        fil[p, TILE + TILE * (n - t) + d, :, lanes] for d in range(1 - TILE, TILE)
                    ]
                    for i in range(TILE):
                        at = (p * 2 + q) * TILE + i
                        for j in range(TILE):
                            sums[at] = sums[at] + left[j] * right[i - j + TILE - 1]
            return tuple(sums)

        zero = jnp.zeros((OWN, 128), F32)
        sums = lax.fori_loop(0, n + 1, step, (zero,) * (6 * TILE))
        one, two, three = (
            jnp.concatenate(
                [jnp.concatenate(sums[(2 * p + q) * TILE : (2 * p + q + 1) * TILE], axis=0) for q in range(2)],
                axis=1,
            )
            for p in range(3)
        )
        prod = jnp.concatenate([one - two, three - one - two], axis=1).astype(BF16)
        if n == 0:
            loads[4].wait()
        back = jnp.dot(prod, bwd[...], preferred_element_type=F32).reshape(TILE, OWN, 2 * ROWS)
        conv = back[:, :, :ROWS] + jnp.concatenate([last, back[:-1, :, ROWS:]], axis=0)
        last = back[TILE - 1 :, :, ROWS:]
        send2[tile] = jnp.concatenate([conv[:, :, :128], conv[:, :, 128:]], axis=1).astype(BF16)
        for to in range(TILE * n, TILE * (n + 1)):
            @pl.when(to != c)
            def _():
                pltpu.make_async_remote_copy(
                    src_ref=send2.at[to], dst_ref=recv2.at[0, c], send_sem=send_sem.at[1],
                    recv_sem=recv2_sem.at[0], device_id=(to, h), device_id_type=MESH,
                ).start()

            @pl.when(to == c)
            def _():
                pltpu.make_async_copy(send2.at[to], recv2.at[0, c], recv2_sem.at[0]).start()

            pltpu.make_async_remote_copy(
                src_ref=send2.at[to], dst_ref=recv2.at[1, c], send_sem=send_sem.at[2],
                recv_sem=recv2_sem.at[1], device_id=(to, sibling[1]), device_id_type=MESH,
            ).start()


    loads[5].wait()
    loads[6].wait()
    for copy in streams:
        copy.wait_recv()
    for s in range(2):
        pltpu.make_async_copy(send2, recv2.at[s], recv2_sem.at[s]).wait()
        returned = recv2[s].astype(F32)
        for i in range(2):
            rows = slice(128 * i, 128 * i + 128)
            conv_t = returned[:, OWN * i : OWN * (i + 1), :].reshape(WIDTH, 128).T
            mixed = key[s, rows].astype(F32) * value[s, rows].astype(F32)
            summed = conv_t + skip[s] * mixed
            gated[rows, WIDTH * s : WIDTH * (s + 1)] = (gate[s, rows].astype(F32) * summed).astype(BF16)

    pltpu.make_async_copy(weight.at[:, pl.ds(0, WIDTH)], weight.at[:, pl.ds(0, WIDTH)], w_sem).wait()
    waitw = pltpu.make_async_remote_copy(
        src_ref=weight.at[:, pl.ds(0, WIDTH)], dst_ref=weight.at[:, pl.ds(WIDTH, WIDTH)],
        send_sem=wsend_sem, recv_sem=wrecv_sem, device_id=sibling, device_id_type=MESH,
    )
    waitw.wait_recv()

    def block(d, y, rows=slice(None)):
        return jnp.dot(
            gated[rows], weight[((x + d) % NX) * 2 + y], preferred_element_type=F32
        )

    order = (2, 1, 3)
    step = ROWS // CHUNKS
    half = ROWS // 2
    top, bottom = slice(0, half), slice(half, ROWS)

    def send_across(r):
        rows = pl.ds(step * r, step)
        copies = []
        for k, d in enumerate(order):
            part[k, rows] = block(d, 1 - yhi, rows).astype(BF16)
            copy = pltpu.make_async_remote_copy(
                src_ref=part.at[k, rows], dst_ref=got.at[k, rows], send_sem=xsend_sem.at[k, r],
                recv_sem=xrecv_sem.at[k, r], device_id=along_x(d), device_id_type=MESH,
            )
            copy.start()
            copies.append(copy)
        return copies

    def send_ring(i, terms):
        ring[i] = terms.astype(BF16)
        copy = pltpu.make_async_remote_copy(
            src_ref=ring.at[i], dst_ref=ringgot.at[i], send_sem=rsend_sem.at[i],
            recv_sem=rrecv_sem.at[i], device_id=along_x(3 if i % 2 else 1), device_id_type=MESH,
        )
        copy.start()
        return copy

    def arrived(i):
        ringcopies[i].wait_recv()
        return ringgot[i].astype(F32)

    first = [send_across(r) for r in range(CHUNKS)]
    far = block(2, yhi)
    ringcopies = [send_ring(0, far[top]), send_ring(1, far[bottom])]
    right, left = block(1, yhi), block(3, yhi)
    ringcopies += [send_ring(2, right[bottom]), send_ring(3, left[top])]
    onward[0] = right[top]
    onward[1] = left[bottom]
    own[0] = block(0, 1 - yhi)
    own[1] = block(0, yhi)
    ycopies = []
    for r in range(CHUNKS):
        rows = pl.ds(step * r, step)
        total = own[0, rows]
        for k in range(NX - 1):
            first[r][k].wait_recv()
            total = total + got[k, rows].astype(F32)
        ypart[rows] = total.astype(BF16)
        copy = pltpu.make_async_remote_copy(
            src_ref=ypart.at[rows], dst_ref=ygot.at[rows], send_sem=ysend_sem.at[r],
            recv_sem=yrecv_sem.at[r], device_id=across, device_id_type=MESH,
        )
        copy.start()
        ycopies.append(copy)
    ringcopies += [send_ring(4 + i, onward[i] + arrived(i)) for i in range(2)]
    own[1, top] = own[1, top] + arrived(3) + arrived(4)
    own[1, bottom] = own[1, bottom] + arrived(2) + arrived(5)
    for r in range(CHUNKS):
        rows = pl.ds(step * r, step)
        ycopies[r].wait_recv()
        out_ref[rows] = (own[1, rows] + ygot[rows].astype(F32)).astype(BF16)

    for n, count in enumerate((CTX - 1, CTX - 1, CTX)):
        sent = (send1, send2, send2)[n].at[pl.ds(0, count)]
        pltpu.make_async_remote_copy(
            src_ref=sent, dst_ref=sent, send_sem=send_sem.at[n], recv_sem=recv2_sem.at[0],
            device_id=sibling, device_id_type=MESH,
        ).wait_send()
    waitw.wait_send()
    for copy in streams + sum(first, []) + ringcopies + ycopies:
        copy.wait_send()


def per_device(gate_stream, key_stream, value_stream, filters, skip_gain, out_weight):
    fwd, bwd = tables()
    any_spec = pl.BlockSpec(memory_space=pl.ANY)
    dma = pltpu.SemaphoreType.DMA
    return pl.pallas_call(
        kernel,
        name="hyena",
        out_shape=pltpu.VMEM((ROWS, WIDTH), BF16),
        in_specs=[any_spec] * 8,
        out_specs=pl.BlockSpec(memory_space=pltpu.VMEM),
        scratch_shapes=[
            pltpu.VMEM((2, ROWS, WIDTH), BF16),
            pltpu.VMEM((2, ROWS, WIDTH), BF16),
            pltpu.VMEM((2, ROWS, WIDTH), BF16),
            pltpu.VMEM((ROWS, WIDTH), F32),
            pltpu.VMEM((2, 1, WIDTH), F32),
            pltpu.VMEM((ROWS, 2 * ROWS), BF16),
            pltpu.VMEM((2 * ROWS, 2 * ROWS), BF16),
            pltpu.VMEM((CTX, 2 * OWN, ROWS), BF16),
            pltpu.VMEM((CTX, 2 * OWN, ROWS), BF16),
            pltpu.VMEM((3, CTX, OWN, ROWS), F32),
            pltpu.VMEM((3, TILE + CTX, OWN, ROWS), F32),
            pltpu.VMEM((CTX, 2 * OWN, 128), BF16),
            pltpu.VMEM((2, CTX, 2 * OWN, 128), BF16),
            pltpu.VMEM((ROWS, 2 * WIDTH), BF16),
            pltpu.VMEM((2 * NX, 2 * WIDTH, WIDTH), BF16),
            pltpu.VMEM((NX - 1, ROWS, WIDTH), BF16),
            pltpu.VMEM((NX - 1, ROWS, WIDTH), BF16),
            pltpu.VMEM((6, ROWS // 2, WIDTH), BF16),
            pltpu.VMEM((6, ROWS // 2, WIDTH), BF16),
            pltpu.VMEM((2, ROWS // 2, WIDTH), F32),
            pltpu.VMEM((2, ROWS, WIDTH), F32),
            pltpu.VMEM((ROWS, WIDTH), BF16),
            pltpu.VMEM((ROWS, WIDTH), BF16),
            dma((7,)), dma, dma, dma, dma((3,)), dma((CTX // TILE,)), dma((2,)), dma((4,)), dma((4,)),
            dma((NX - 1, CHUNKS)), dma((NX - 1, CHUNKS)), dma((6,)), dma((6,)), dma((CHUNKS,)), dma((CHUNKS,)),
        ],
        compiler_params=pltpu.CompilerParams(
            collective_id=0, has_side_effects=True, vmem_limit_bytes=56 << 20
        ),
    )(
        gate_stream, key_stream, value_stream, filters, skip_gain[None, :], out_weight,
        jnp.asarray(fwd), jnp.asarray(bwd),
    )


def solution(mesh):
    return jax.shard_map(
        per_device,
        mesh=mesh,
        in_specs=(
            P("ctx", "ch"),
            P("ctx", "ch"),
            P("ctx", "ch"),
            P("ctx", "ch"),
            P("ch"),
            P("ch", None),
        ),
        out_specs=P("ctx", "ch"),
        check_vma=False,
    )
```

```python
import functools
import math

import jax
import jax.numpy as jnp
import numpy as np
from jax import lax
from jax.experimental import pallas as pl
from jax.experimental.pallas import tpu as pltpu
from jax.sharding import PartitionSpec as P

MESH = pl.DeviceIdType.MESH
F32 = jnp.float32
BF16 = jnp.bfloat16

CTX = 32
ROWS = 256
WIDTH = 256
OWN = WIDTH // CTX
NX = 4
SIZES = (64, 64, 64, 32)
MAIN = sum(SIZES)
REST = ROWS - MAIN
STRIDE = 5
MID = 3
TILE = 4


def tables():
    freq = np.arange(ROWS) + 0.5
    pos = np.arange(2 * ROWS)
    theta = 2.0 * math.pi * pos[:, None] * freq[None, :] / (2 * ROWS)
    forward = np.concatenate([np.cos(theta[:ROWS]), -np.sin(theta[:ROWS])], axis=1)
    backward = np.concatenate([np.cos(theta.T), -np.sin(theta.T)], axis=0) / ROWS
    return forward.astype(BF16), backward.astype(BF16)


def kernel(
    gate_hbm, key_hbm, value_hbm, filters_hbm, skip_hbm, weight_hbm, fwd_hbm, bwd_hbm,
    out_ref,
    gate, key, value, filters, skip, fwd, bwd,
    send1, recv1, sig, fil, send2, recv2,
    gated, weight, part, got, ring, ringgot, onward, own, ypart, ygot, ahead, aheadgot, onrest,
    in_sem, w_sem, wsend_sem, wrecv_sem, send_sem, recv_sem, recv2_sem, gsend_sem, grecv_sem,
    xsend_sem, xrecv_sem, rsend_sem, rrecv_sem, ysend_sem, yrecv_sem,
):
    c = lax.axis_index("ctx")
    h = lax.axis_index("ch")
    x = h // 4
    yhi = (h // 2) % 2
    core = h % 2
    sibling = (c, h + 1 - 2 * core)
    across = (c, h + 2 - 4 * yhi)

    def along_x(d):
        return (c, ((x + d) % NX) * 4 + yhi * 2 + core)

    barrier = pltpu.get_barrier_semaphore()

    def greet(k, carry):
        pl.semaphore_signal(barrier, inc=1, device_id=((c + k) % CTX, h), device_id_type=MESH)
        return carry

    lax.fori_loop(1, CTX, greet, 0, unroll=True)
    others = [sibling, across] + [along_x(d) for d in range(1, NX)]
    for dev in others:
        pl.semaphore_signal(barrier, inc=1, device_id=dev, device_id_type=MESH)

    loads = []
    for i, (src, dst) in enumerate(
        [(key_hbm, key.at[0]), (value_hbm, value.at[0]), (filters_hbm, filters), (fwd_hbm, fwd),
         (bwd_hbm, bwd), (gate_hbm, gate.at[0]), (skip_hbm, skip.at[0])]
    ):
        load = pltpu.make_async_copy(src, dst, in_sem.at[i])
        load.start()
        loads.append(load)

    for i in range(2 * NX):
        copy = pltpu.make_async_copy(
            weight_hbm.at[:, pl.ds(pl.multiple_of((2 * i + core) * WIDTH, WIDTH), WIDTH)],
            weight.at[i, pl.ds(0, WIDTH)],
            w_sem,
        )
        copy.start()

    loads[0].wait()
    loads[1].wait()
    mixed = key[0].astype(F32) * value[0].astype(F32)
    loads[2].wait()
    mixed_t = mixed.T.reshape(CTX, OWN, ROWS)
    filters_t = filters[...].T.reshape(CTX, OWN, ROWS)
    send1[...] = jnp.concatenate([mixed_t, filters_t], axis=1).astype(BF16)
    pltpu.make_async_copy(send1.at[c], recv1.at[c], recv_sem.at[c // TILE]).start()

    pl.semaphore_wait(barrier, CTX - 1 + len(others))

    for k in range(1, CTX):
        to = (c + k * STRIDE % CTX) % CTX
        pltpu.make_async_remote_copy(
            src_ref=send1.at[to], dst_ref=recv1.at[c], send_sem=send_sem.at[0],
            recv_sem=recv_sem.at[c // TILE], device_id=(to, h), device_id_type=MESH,
        ).start()

    for i in range(2 * NX):
        pltpu.make_async_remote_copy(
            src_ref=weight_hbm.at[:, pl.ds(pl.multiple_of((2 * i + 1 - core) * WIDTH, WIDTH), WIDTH)],
            dst_ref=weight.at[i, pl.ds(WIDTH, WIDTH)],
            send_sem=wsend_sem, recv_sem=wrecv_sem, device_id=sibling, device_id_type=MESH,
        ).start()
    streams = [
        pltpu.make_async_remote_copy(
            src_ref=src, dst_ref=dst.at[1], send_sem=gsend_sem.at[i], recv_sem=grecv_sem.at[i],
            device_id=sibling, device_id_type=MESH,
        )
        for i, (src, dst) in enumerate(
            [(key_hbm, key), (value_hbm, value), (gate_hbm, gate), (skip_hbm, skip)]
        )
    ]
    for copy in streams:
        copy.start()

    loads[3].wait()
    fil[:, 0:TILE] = jnp.zeros((3, TILE, OWN, ROWS), F32)
    last = jnp.zeros((1, OWN, ROWS), F32)
    for n in range(CTX // TILE):
        tile = pl.ds(TILE * n, TILE)
        pltpu.make_async_copy(send1.at[tile], recv1.at[tile], recv_sem.at[n]).wait()
        spec = jnp.dot(
            recv1[tile].reshape(TILE * 2 * OWN, ROWS), fwd[...], preferred_element_type=F32
        ).reshape(TILE, 2 * OWN, 2 * ROWS)
        for ref, start, low in ((sig, 0, 0), (fil, TILE, OWN)):
            real = spec[:, low : low + OWN, :ROWS]
            imag = spec[:, low : low + OWN, ROWS:]
            ref[0, pl.ds(start + TILE * n, TILE)] = real
            ref[1, pl.ds(start + TILE * n, TILE)] = imag
            ref[2, pl.ds(start + TILE * n, TILE)] = real + imag

        def step(t, sums):
            sums = list(sums)
            for p in range(3):
                for q in range(2):
                    lanes = slice(128 * q, 128 * q + 128)
                    left = [sig[p, TILE * t + j, :, lanes] for j in range(TILE)]
                    right = [
                        fil[p, TILE + TILE * (n - t) + d, :, lanes] for d in range(1 - TILE, TILE)
                    ]
                    for i in range(TILE):
                        at = (p * 2 + q) * TILE + i
                        for j in range(TILE):
                            sums[at] = sums[at] + left[j] * right[i - j + TILE - 1]
            return tuple(sums)

        zero = jnp.zeros((OWN, 128), F32)
        sums = lax.fori_loop(0, n + 1, step, (zero,) * (6 * TILE))
        one, two, three = (
            jnp.concatenate(
                [jnp.concatenate(sums[(2 * p + q) * TILE : (2 * p + q + 1) * TILE], axis=0) for q in range(2)],
                axis=1,
            )
            for p in range(3)
        )
        prod = jnp.concatenate([one - two, three - one - two], axis=1).astype(BF16)
        if n == 0:
            loads[4].wait()
        back = jnp.dot(prod, bwd[...], preferred_element_type=F32).reshape(TILE, OWN, 2 * ROWS)
        conv = back[:, :, :ROWS] + jnp.concatenate([last, back[:-1, :, ROWS:]], axis=0)
        last = back[TILE - 1 :, :, ROWS:]
        send2[tile] = jnp.concatenate([conv[:, :, :128], conv[:, :, 128:]], axis=1).astype(BF16)
        for to in range(TILE * n, TILE * (n + 1)):
            @pl.when(to != c)
            def _():
                pltpu.make_async_remote_copy(
                    src_ref=send2.at[to], dst_ref=recv2.at[0, c], send_sem=send_sem.at[1],
                    recv_sem=recv2_sem.at[0], device_id=(to, h), device_id_type=MESH,
                ).start()

            @pl.when(to == c)
            def _():
                pltpu.make_async_copy(send2.at[to], recv2.at[0, c], recv2_sem.at[0]).start()

            pltpu.make_async_remote_copy(
                src_ref=send2.at[to], dst_ref=recv2.at[1, c], send_sem=send_sem.at[2],
                recv_sem=recv2_sem.at[1], device_id=(to, sibling[1]), device_id_type=MESH,
            ).start()


    loads[5].wait()
    loads[6].wait()
    for copy in streams:
        copy.wait_recv()
    for s in range(2):
        pltpu.make_async_copy(send2, recv2.at[s], recv2_sem.at[s]).wait()
        returned = recv2[s].astype(F32)
        for i in range(2):
            rows = slice(128 * i, 128 * i + 128)
            conv_t = returned[:, OWN * i : OWN * (i + 1), :].reshape(WIDTH, 128).T
            mixed = key[s, rows].astype(F32) * value[s, rows].astype(F32)
            summed = conv_t + skip[s] * mixed
            gated[rows, WIDTH * s : WIDTH * (s + 1)] = (gate[s, rows].astype(F32) * summed).astype(BF16)

    pltpu.make_async_copy(weight.at[:, pl.ds(0, WIDTH)], weight.at[:, pl.ds(0, WIDTH)], w_sem).wait()
    waitw = pltpu.make_async_remote_copy(
        src_ref=weight.at[:, pl.ds(0, WIDTH)], dst_ref=weight.at[:, pl.ds(WIDTH, WIDTH)],
        send_sem=wsend_sem, recv_sem=wrecv_sem, device_id=sibling, device_id_type=MESH,
    )
    waitw.wait_recv()

    def block(d, y, rows=slice(None)):
        return jnp.dot(
            gated[rows], weight[((x + d) % NX) * 2 + y], preferred_element_type=F32
        )

    order = (2, 1, 3)
    half = MAIN // 2
    top, bottom, rest = slice(0, half), slice(half, MAIN), slice(MAIN, ROWS)

    def chunk(r):
        return pl.ds(sum(SIZES[:r]), SIZES[r])

    def send_across(r):
        rows = chunk(r)
        copies = []
        for k, d in enumerate(order):
            part[k, rows] = block(d, 1 - yhi, rows).astype(BF16)
            copy = pltpu.make_async_remote_copy(
                src_ref=part.at[k, rows], dst_ref=got.at[k, rows], send_sem=xsend_sem.at[k, r],
                recv_sem=xrecv_sem.at[k, r], device_id=along_x(d), device_id_type=MESH,
            )
            copy.start()
            copies.append(copy)
        return copies

    def send_ring(i, terms):
        ring[i] = terms.astype(BF16)
        copy = pltpu.make_async_remote_copy(
            src_ref=ring.at[i], dst_ref=ringgot.at[i], send_sem=rsend_sem.at[i],
            recv_sem=rrecv_sem.at[i], device_id=along_x(3 if i % 2 else 1), device_id_type=MESH,
        )
        copy.start()
        return copy

    def arrived(i):
        ringcopies[i].wait_recv()
        return ringgot[i].astype(F32)

    for d in range(NX):
        ahead[d] = block(d, 1 - yhi, rest).astype(BF16)
    aheadcopy = pltpu.make_async_remote_copy(
        src_ref=ahead, dst_ref=aheadgot, send_sem=ysend_sem.at[len(SIZES)],
        recv_sem=yrecv_sem.at[len(SIZES)], device_id=across, device_id_type=MESH,
    )
    aheadcopy.start()
    first = [send_across(r) for r in range(len(SIZES))]
    far = block(2, yhi)
    ringcopies = [send_ring(0, far[top]), send_ring(1, far[bottom])]
    right, left = block(1, yhi), block(3, yhi)
    ringcopies += [send_ring(2, right[bottom]), send_ring(3, left[top])]
    onward[0] = right[top]
    onward[1] = left[bottom]
    own[0] = block(0, 1 - yhi)
    for d, terms in ((1, right), (2, far), (3, left)):
        onrest[d - 1] = terms[rest]
    own[1] = block(0, yhi)
    ycopies = [aheadcopy]
    restcopies = []

    def send_rest():
        aheadcopy.wait_recv()
        for k, d in enumerate(order):
            part[k, rest] = (onrest[d - 1] + aheadgot[d].astype(F32)).astype(BF16)
            copy = pltpu.make_async_remote_copy(
                src_ref=part.at[k, pl.ds(MAIN, REST)], dst_ref=got.at[k, pl.ds(MAIN, REST)],
                send_sem=xsend_sem.at[k, len(SIZES)], recv_sem=xrecv_sem.at[k, len(SIZES)],
                device_id=along_x(d), device_id_type=MESH,
            )
            copy.start()
            restcopies.append(copy)

    for r in range(len(SIZES)):
        if r == MID:
            send_rest()
        rows = chunk(r)
        total = own[0, rows]
        for k in range(NX - 1):
            first[r][k].wait_recv()
            total = total + got[k, rows].astype(F32)
        ypart[rows] = total.astype(BF16)
        copy = pltpu.make_async_remote_copy(
            src_ref=ypart.at[rows], dst_ref=ygot.at[rows], send_sem=ysend_sem.at[r],
            recv_sem=yrecv_sem.at[r], device_id=across, device_id_type=MESH,
        )
        copy.start()
        ycopies.append(copy)
    ringcopies += [send_ring(4 + i, onward[i] + arrived(i)) for i in range(2)]
    own[1, top] = own[1, top] + arrived(3) + arrived(4)
    own[1, bottom] = own[1, bottom] + arrived(2) + arrived(5)
    total = own[1, rest] + aheadgot[0].astype(F32)
    for k in range(NX - 1):
        restcopies[k].wait_recv()
        total = total + got[k, rest].astype(F32)
    out_ref[rest] = total.astype(BF16)
    for r in range(len(SIZES)):
        rows = chunk(r)
        ycopies[r + 1].wait_recv()
        out_ref[rows] = (own[1, rows] + ygot[rows].astype(F32)).astype(BF16)

    for n, count in enumerate((CTX - 1, CTX - 1, CTX)):
        sent = (send1, send2, send2)[n].at[pl.ds(0, count)]
        pltpu.make_async_remote_copy(
            src_ref=sent, dst_ref=sent, send_sem=send_sem.at[n], recv_sem=recv2_sem.at[0],
            device_id=sibling, device_id_type=MESH,
        ).wait_send()
    waitw.wait_send()
    for copy in streams + sum(first, []) + ringcopies + ycopies + restcopies:
        copy.wait_send()


def per_device(gate_stream, key_stream, value_stream, filters, skip_gain, out_weight):
    fwd, bwd = tables()
    any_spec = pl.BlockSpec(memory_space=pl.ANY)
    dma = pltpu.SemaphoreType.DMA
    return pl.pallas_call(
        kernel,
        name="hyena",
        out_shape=pltpu.VMEM((ROWS, WIDTH), BF16),
        in_specs=[any_spec] * 8,
        out_specs=pl.BlockSpec(memory_space=pltpu.VMEM),
        scratch_shapes=[
            pltpu.VMEM((2, ROWS, WIDTH), BF16),
            pltpu.VMEM((2, ROWS, WIDTH), BF16),
            pltpu.VMEM((2, ROWS, WIDTH), BF16),
            pltpu.VMEM((ROWS, WIDTH), F32),
            pltpu.VMEM((2, 1, WIDTH), F32),
            pltpu.VMEM((ROWS, 2 * ROWS), BF16),
            pltpu.VMEM((2 * ROWS, 2 * ROWS), BF16),
            pltpu.VMEM((CTX, 2 * OWN, ROWS), BF16),
            pltpu.VMEM((CTX, 2 * OWN, ROWS), BF16),
            pltpu.VMEM((3, CTX, OWN, ROWS), F32),
            pltpu.VMEM((3, TILE + CTX, OWN, ROWS), F32),
            pltpu.VMEM((CTX, 2 * OWN, 128), BF16),
            pltpu.VMEM((2, CTX, 2 * OWN, 128), BF16),
            pltpu.VMEM((ROWS, 2 * WIDTH), BF16),
            pltpu.VMEM((2 * NX, 2 * WIDTH, WIDTH), BF16),
            pltpu.VMEM((NX - 1, ROWS, WIDTH), BF16),
            pltpu.VMEM((NX - 1, ROWS, WIDTH), BF16),
            pltpu.VMEM((6, MAIN // 2, WIDTH), BF16),
            pltpu.VMEM((6, MAIN // 2, WIDTH), BF16),
            pltpu.VMEM((2, MAIN // 2, WIDTH), F32),
            pltpu.VMEM((2, ROWS, WIDTH), F32),
            pltpu.VMEM((ROWS, WIDTH), BF16),
            pltpu.VMEM((ROWS, WIDTH), BF16),
            pltpu.VMEM((NX, REST, WIDTH), BF16),
            pltpu.VMEM((NX, REST, WIDTH), BF16),
            pltpu.VMEM((NX - 1, REST, WIDTH), F32),
            dma((7,)), dma, dma, dma, dma((3,)), dma((CTX // TILE,)), dma((2,)), dma((4,)), dma((4,)),
            dma((NX - 1, len(SIZES) + 1)), dma((NX - 1, len(SIZES) + 1)), dma((6,)), dma((6,)), dma((len(SIZES) + 1,)), dma((len(SIZES) + 1,)),
        ],
        compiler_params=pltpu.CompilerParams(
            collective_id=0, has_side_effects=True, vmem_limit_bytes=56 << 20
        ),
    )(
        gate_stream, key_stream, value_stream, filters, skip_gain[None, :], out_weight,
        jnp.asarray(fwd), jnp.asarray(bwd),
    )


def solution(mesh):
    return jax.shard_map(
        per_device,
        mesh=mesh,
        in_specs=(
            P("ctx", "ch"),
            P("ctx", "ch"),
            P("ctx", "ch"),
            P("ctx", "ch"),
            P("ch"),
            P("ch", None),
        ),
        out_specs=P("ctx", "ch"),
        check_vma=False,
    )
```
